32 devices in a mesh: fsdp: 16 (over z, x, core), tp: 2 (over y).
Axes of the slice: x: 2, y: 2, z: 4, core: 2. Of those that a mesh axis runs over, the one named last changes fastest.
Arguments:
- hidden: bfloat16 [1024, 26624], P('fsdp', 'tp'), may hold values from -6 to 6
- out_grad: bfloat16 [1024, 16384], P('tp', 'fsdp'), may hold values from -6 to 6
- weight: bfloat16 [26624, 16384], P('tp', 'fsdp'), may hold values from -0.0390625 to 0.0390625
Outputs:
- hidden_grad: bfloat16 [1024, 26624], P('fsdp', 'tp')
- weight_grad: float32 [26624, 16384], P('tp', 'fsdp')
The draws below stay inside these ranges and needn't reach their ends.
All inputs are finite; a program needn't handle non-finite values.
Results may differ from the reference program's by a relative error of at most 0.015.
Values may be sent and summed in bfloat16 or wider, within the bound.
A program may use at most 192 MiB of HBM per device.

```python
import math
import jax
import jax.numpy as jnp
from jax import lax

D = 16384
FF = 26624
TOKENS = 1024
N_FSDP = 16


def with_spikes(result, rng, source, target, blocks, factor):
    owner, partner = [(jnp.arange(result.shape[axis_at]) // (result.shape[axis_at] // blocks)).reshape([-1 if axis == axis_at else 1 for axis in range(result.ndim)]) for axis_at in (source, target)]
    chosen = jax.random.permutation(rng, blocks)[partner]
    strong = (owner == chosen) | (owner == (partner + blocks // 2) % blocks)
    return jnp.where(strong, factor * result, result)


def steps_of(own_key, extent, pieces, smallest, high):
    def one(position, shards_of):
        draws = jax.random.uniform(jax.random.fold_in(jax.random.fold_in(own_key, 6), position), (shards_of,), jnp.float32, smallest / len(pieces), high / len(pieces))
        return jnp.repeat(jnp.exp(draws), extent[position] // shards_of).reshape((-1,) + (1,) * (len(extent) - position - 1))

    gain = one(*pieces[0])
    for cut in pieces[1:]:
        gain = gain * one(*cut)
    return gain


def gaussian(key, dims, width, limit, pieces=(), held_as=jnp.bfloat16):
    result = jax.random.normal(key, dims, jnp.float32) * width
    if len(pieces) > 0:
        result = steps_of(key, dims, pieces, -0.22, 0.18) * result
    return jnp.clip(result, min=-limit, max=limit).astype(held_as)


def gaussian_with(stream_key, shape, scale, most, split, heavy, held_as=jnp.bfloat16):
    drawn = scale * jax.random.normal(stream_key, shape, jnp.float32)
    if split:
        drawn = drawn * steps_of(stream_key, shape, split, -0.22, 0.18)
    return jnp.clip(with_spikes(drawn, jax.random.fold_in(stream_key, 3), *heavy), -most, most).astype(held_as)


def setup_inputs(seed: int = 0) -> dict:
    streams_of = jax.random.split(jax.random.key(seed), 4)
    hidden = gaussian(streams_of[0], (TOKENS, FF), 1.0, 6.0, ((0, 16), (1, 2)))
    out_grad = gaussian_with(streams_of[1], (TOKENS, D), 1.0, 6.0, ((0, 2), (1, 16)), (1, 0, 16, 2.0))
    weight = gaussian(streams_of[2], (FF, D), FF ** -0.5, 0.0390625, ((0, 2), (1, 16)))
    return dict(hidden=hidden, out_grad=out_grad, weight=weight)


def reference(hidden, out_grad, weight):
    block = D // N_FSDP
    grad_blocks = out_grad.reshape(TOKENS, N_FSDP, block).transpose(1, 0, 2)
    weight_blocks = weight.reshape(FF, N_FSDP, block).transpose(1, 0, 2)

    def add_block(running, pair):
        term = lax.dot_general(pair[0], pair[1], (((1,), (1,)), ((), ())), preferred_element_type=jnp.float32)
        rounded = lax.optimization_barrier(term.astype(jnp.bfloat16))
        return (running + rounded.astype(jnp.float32), None)
    adjoint, unused = lax.scan(add_block, jnp.zeros((TOKENS, FF), jnp.float32), (grad_blocks, weight_blocks))
    hidden_grad = (adjoint + 0.5 * hidden.astype(jnp.float32)).astype(jnp.bfloat16)
    weight_grad = lax.dot_general(hidden, out_grad, (((0,), (0,)), ((), ())), preferred_element_type=jnp.float32)
    weight_grad = weight_grad * (1.0 / math.sqrt(TOKENS))
    return (hidden_grad, weight_grad)
```

```python
import math

import jax
import jax.numpy as jnp
import numpy as np
from jax import lax
from jax.sharding import PartitionSpec as P

SUB = 2


def ring_of(chips):
    order = list(range(0, chips, 2))
    order += [c for c in range(chips - 1, -1, -1) if c % 2 == 1]
    return order


def local(n, n_tp, hidden, out_grad, weight):
    chips = n // 2
    ring = ring_of(chips)
    place = [0] * chips
    for at, chip in enumerate(ring):
        place[chip] = at
    table = np.zeros((n, 2, chips), np.int32)
    for i in range(n):
        for d, step in enumerate((1, -1)):
            table[i, d] = [ring[(place[i // 2] - step * s) % chips] for s in range(chips)]
    me = lax.axis_index("fsdp")
    core = lax.rem(me, 2)
    behind = lax.dynamic_slice(
        jnp.asarray(table), (me, 0, 0), (1, 2, chips), allow_negative_indices=False
    )

    def chip_behind(step, s):
        return behind[0, 0 if step == 1 else 1, s]

    def put(into, block, at):
        start = (at,) + (0,) * block.ndim
        return lax.dynamic_update_slice(into, block[None], start, allow_negative_indices=False)

    def take(whole, at):
        start = (at,) + (0,) * (whole.ndim - 1)
        return lax.dynamic_slice(
            whole, start, (1,) + whole.shape[1:], allow_negative_indices=False
        )[0]

    def shift(value, step):
        pairs = []
        for i in range(chips):
            for c in range(2):
                pairs.append((ring[i] * 2 + c, ring[(i + step) % chips] * 2 + c))
        return lax.ppermute(value, "fsdp", pairs)

    def swap(value):
        return lax.ppermute(value, "fsdp", [(i, i ^ 1) for i in range(n)])

    rows, width = hidden.shape
    piece = width // (2 * SUB)
    chains = [(k * piece, 1 if k % 2 == 0 else -1) for k in range(2 * SUB)]

    tp_at = lax.axis_index("tp")
    part = out_grad.shape[0]
    grad_rows = jnp.zeros((n_tp,) + out_grad.shape, out_grad.dtype)
    grad_rows = put(grad_rows, out_grad, tp_at)
    for i in range(1, n_tp):
        other = lax.ppermute(out_grad, "tp", [(j, (j + i) % n_tp) for j in range(n_tp)])
        grad_rows = put(grad_rows, other, lax.rem(tp_at - i + n_tp, n_tp))
    grad_rows = grad_rows.reshape(n_tp * part, -1)

    held = [hidden[:, c : c + piece] for c, _ in chains]
    own = list(held)
    gathered = [jnp.zeros((n, rows, piece), hidden.dtype) for _ in chains]
    for k, block in enumerate(held):
        gathered[k] = put(gathered[k], block, me)
        gathered[k] = put(gathered[k], swap(block), me + 1 - 2 * core)
    for s in range(1, chips):
        for k, (_, step) in enumerate(chains):
            held[k] = shift(held[k], step)
            owner = chip_behind(step, s) * 2
            gathered[k] = put(gathered[k], held[k], owner + core)
            gathered[k] = put(gathered[k], swap(held[k]), owner + 1 - core)

    split = grad_rows.reshape(chips, 2, rows, -1).transpose(1, 0, 2, 3)
    nt = (((1,), (1,)), ((), ()))

    def partial(c, k):
        first = chains[k][0]
        mine = take(split, c).reshape(chips * rows, -1)
        out = lax.dot_general(
            mine, weight[first : first + piece], nt, preferred_element_type=jnp.float32
        )
        return out.astype(jnp.bfloat16).reshape(chips, rows, piece)

    theirs = [swap(partial(1 - core, k)) for k in range(len(chains))]
    ours = [partial(core, k) for k in range(len(chains))]

    def term(k, chip):
        return take(ours[k], chip).astype(jnp.float32) + take(theirs[k], chip).astype(jnp.float32)

    sums = []
    for k, (_, step) in enumerate(chains):
        first = term(k, chip_behind(step, 1)).astype(jnp.bfloat16)
        first, held[k] = lax.optimization_barrier((first, held[k]))
        sums.append(first)
    scale = 1.0 / math.sqrt(grad_rows.shape[0])
    weight_grad = jnp.zeros((width, grad_rows.shape[1]), jnp.float32)
    tn = (((0,), (0,)), ((), ()))
    for s in range(1, chips):
        for k, (_, step) in enumerate(chains):
            total = shift(sums[k], step).astype(jnp.float32)
            total = total + term(k, chip_behind(step, (s + 1) % chips))
            if s == chips - 1:
                total = total + 0.5 * own[k].astype(jnp.float32)
            sums[k] = total.astype(jnp.bfloat16)
        if s <= len(chains):
            k = s - 1
            sums[k], block = lax.optimization_barrier((sums[k], gathered[k]))
            block = lax.dot_general(
                block.reshape(n * rows, piece), grad_rows, tn, preferred_element_type=jnp.float32
            )
            weight_grad = lax.dynamic_update_slice(weight_grad, block * scale, (chains[k][0], 0))
    hidden_grad = jnp.concatenate(sums, axis=1)
    return (hidden_grad, weight_grad)


def solution(mesh):
    n, n_tp = mesh.shape["fsdp"], mesh.shape["tp"]
    placed = (P("fsdp", "tp"), P("tp", "fsdp"), P("tp", "fsdp"))
    return jax.shard_map(
        lambda *args: local(n, n_tp, *args),
        mesh=mesh,
        in_specs=placed,
        out_specs=(P("fsdp", "tp"), P("tp", "fsdp")),
        check_vma=False,
    )
```

```python
import math

import jax
import jax.numpy as jnp
import numpy as np
from jax import lax
from jax.sharding import PartitionSpec as P

SUB = 2


def ring_of(chips):
    order = list(range(0, chips, 2))
    order += [c for c in range(chips - 1, -1, -1) if c % 2 == 1]
    return order


def local(n, n_tp, hidden, out_grad, weight):
    chips = n // 2
    ring = ring_of(chips)
    place = [0] * chips
    for at, chip in enumerate(ring):
        place[chip] = at
    table = np.zeros((n, 2, chips), np.int32)
    for i in range(n):
        for d, step in enumerate((1, -1)):
            table[i, d] = [ring[(place[i // 2] - step * s) % chips] for s in range(chips)]
    me = lax.axis_index("fsdp")
    core = lax.rem(me, 2)
    behind = lax.dynamic_slice(
        jnp.asarray(table), (me, 0, 0), (1, 2, chips), allow_negative_indices=False
    )

    def chip_behind(step, s):
        return behind[0, 0 if step == 1 else 1, s]

    def put(into, block, at):
        start = (at,) + (0,) * block.ndim
        return lax.dynamic_update_slice(into, block[None], start, allow_negative_indices=False)

    def take(whole, at):
        start = (at,) + (0,) * (whole.ndim - 1)
        return lax.dynamic_slice(
            whole, start, (1,) + whole.shape[1:], allow_negative_indices=False
        )[0]

    def shift(value, step):
        pairs = []
        for i in range(chips):
            for c in range(2):
                pairs.append((ring[i] * 2 + c, ring[(i + step) % chips] * 2 + c))
        return lax.ppermute(value, "fsdp", pairs)

    def swap(value):
        return lax.ppermute(value, "fsdp", [(i, i ^ 1) for i in range(n)])

    rows, width = hidden.shape
    piece = width // (2 * SUB)
    chains = [(k * piece, 1 if k % 2 == 0 else -1) for k in range(2 * SUB)]

    tp_at = lax.axis_index("tp")
    part = out_grad.shape[0]
    grad_rows = jnp.zeros((n_tp,) + out_grad.shape, out_grad.dtype)
    grad_rows = put(grad_rows, out_grad, tp_at)
    for i in range(1, n_tp):
        other = lax.ppermute(out_grad, "tp", [(j, (j + i) % n_tp) for j in range(n_tp)])
        grad_rows = put(grad_rows, other, lax.rem(tp_at - i + n_tp, n_tp))
    grad_rows = grad_rows.reshape(n_tp * part, -1)

    split = grad_rows.reshape(chips, 2, rows, -1).transpose(1, 0, 2, 3)
    ordered = jnp.stack([take(split, 1 - core), take(split, core)]).reshape(n * rows, -1)
    nt = (((1,), (1,)), ((), ()))
    tn = (((0,), (0,)), ((), ()))
    scale = 1.0 / math.sqrt(n * rows)
    weight_grad = jnp.zeros((width, ordered.shape[1]), jnp.float32)

    held = [hidden[:, c : c + piece] for c, _ in chains]
    own = list(held)
    gathered = [jnp.zeros((2, chips, rows, piece), hidden.dtype) for _ in chains]
    my_chip = me // 2

    def keep(into, block, chip):
        return lax.dynamic_update_slice(
            into, block[None, None], (1, chip, 0, 0), allow_negative_indices=False
        )

    gathered = [keep(g, block, my_chip) for g, block in zip(gathered, held)]
    ours, theirs = [], []
    count = len(chains)
    for s in range(1, chips):
        for k, (_, step) in enumerate(chains):
            held[k] = shift(held[k], step)
            gathered[k] = keep(gathered[k], held[k], chip_behind(step, s))
        if s == 1:
            held[0], weight_grad = lax.optimization_barrier((held[0], weight_grad))
        k = s - 3
        if 0 <= k < count:
            held[k], theirs[k] = lax.optimization_barrier((held[k], theirs[k]))
        k = s - 2
        if 0 <= k < count:
            held[k], rows_now = lax.optimization_barrier((held[k], ordered))
            first = chains[k][0]
            out = lax.dot_general(
                rows_now, weight[first : first + piece], nt, preferred_element_type=jnp.float32
            )
            out = out.astype(jnp.bfloat16).reshape(2, chips, rows, piece)
            theirs.append(swap(out[0]))
            ours.append(out[1])

    def term(k, chip):
        return take(ours[k], chip).astype(jnp.float32) + take(theirs[k], chip).astype(jnp.float32)

    sums = []
    for k, (_, step) in enumerate(chains):
        first = term(k, chip_behind(step, 1)).astype(jnp.bfloat16)
        first, held[k] = lax.optimization_barrier((first, held[k]))
        sums.append(first)
    others = []
    for s in range(1, chips):
        for k, (_, step) in enumerate(chains):
            total = shift(sums[k], step).astype(jnp.float32)
            total = total + term(k, chip_behind(step, (s + 1) % chips))
            if s == chips - 1:
                total = total + 0.5 * own[k].astype(jnp.float32)
            sums[k] = total.astype(jnp.bfloat16)
        k = s - 2
        if 0 <= k < count:
            sums[k], block = lax.optimization_barrier((sums[k], others[k]))
            block = gathered[k].at[0].set(block).reshape(n * rows, piece)
            block = lax.dot_general(block, ordered, tn, preferred_element_type=jnp.float32)
            weight_grad = lax.dynamic_update_slice(weight_grad, block * scale, (chains[k][0], 0))
        k = s - 1
        if k < count:
            sums[k], mine = lax.optimization_barrier((sums[k], gathered[k][1]))
            others.append(swap(mine))
    hidden_grad = jnp.concatenate(sums, axis=1)
    return (hidden_grad, weight_grad)


def solution(mesh):
    n, n_tp = mesh.shape["fsdp"], mesh.shape["tp"]
    placed = (P("fsdp", "tp"), P("tp", "fsdp"), P("tp", "fsdp"))
    return jax.shard_map(
        lambda *args: local(n, n_tp, *args),
        mesh=mesh,
        in_specs=placed,
        out_specs=(P("fsdp", "tp"), P("tp", "fsdp")),
        check_vma=False,
    )
```

```python
import math

import jax
import jax.numpy as jnp
import numpy as np
from jax import lax
from jax.sharding import PartitionSpec as P

SUB = 1


def ring_of(chips):
    order = list(range(0, chips, 2))
    order += [c for c in range(chips - 1, -1, -1) if c % 2 == 1]
    return order


def local(n, n_tp, hidden, out_grad, weight):
    chips = n // 2
    ring = ring_of(chips)
    place = [0] * chips
    for at, chip in enumerate(ring):
        place[chip] = at
    table = np.zeros((n, 2, chips), np.int32)
    for i in range(n):
        for d, step in enumerate((1, -1)):
            table[i, d] = [ring[(place[i // 2] - step * s) % chips] for s in range(chips)]
    me = lax.axis_index("fsdp")
    core = lax.rem(me, 2)
    behind = lax.dynamic_slice(
        jnp.asarray(table), (me, 0, 0), (1, 2, chips), allow_negative_indices=False
    )

    def chip_behind(step, s):
        return behind[0, 0 if step == 1 else 1, s]

    def put(into, block, at):
        start = (at,) + (0,) * block.ndim
        return lax.dynamic_update_slice(into, block[None], start, allow_negative_indices=False)

    def take(whole, at):
        start = (at,) + (0,) * (whole.ndim - 1)
        return lax.dynamic_slice(
            whole, start, (1,) + whole.shape[1:], allow_negative_indices=False
        )[0]

    def shift(value, step):
        pairs = []
        for i in range(chips):
            for c in range(2):
                pairs.append((ring[i] * 2 + c, ring[(i + step) % chips] * 2 + c))
        return lax.ppermute(value, "fsdp", pairs)

    def swap(value):
        return lax.ppermute(value, "fsdp", [(i, i ^ 1) for i in range(n)])

    rows, width = hidden.shape
    piece = width // (2 * SUB)
    chains = [(k * piece, 1 if k % 2 == 0 else -1) for k in range(2 * SUB)]

    tp_at = lax.axis_index("tp")
    part = out_grad.shape[0]
    grad_rows = jnp.zeros((n_tp,) + out_grad.shape, out_grad.dtype)
    grad_rows = put(grad_rows, out_grad, tp_at)
    for i in range(1, n_tp):
        other = lax.ppermute(out_grad, "tp", [(j, (j + i) % n_tp) for j in range(n_tp)])
        grad_rows = put(grad_rows, other, lax.rem(tp_at - i + n_tp, n_tp))
    grad_rows = grad_rows.reshape(n_tp * part, -1)

    split = grad_rows.reshape(chips, 2, rows, -1).transpose(1, 0, 2, 3)
    ordered = jnp.stack([take(split, 1 - core), take(split, core)]).reshape(n * rows, -1)
    nt = (((1,), (1,)), ((), ()))
    tn = (((0,), (0,)), ((), ()))
    scale = 1.0 / math.sqrt(n * rows)
    weight_grad = jnp.zeros((width, ordered.shape[1]), jnp.float32)

    held = [hidden[:, c : c + piece] for c, _ in chains]
    own = list(held)
    gathered = [jnp.zeros((2, chips, rows, piece), hidden.dtype) for _ in chains]
    my_chip = me // 2

    def keep(into, block, chip):
        return lax.dynamic_update_slice(
            into, block[None, None], (1, chip, 0, 0), allow_negative_indices=False
        )

    gathered = [keep(g, block, my_chip) for g, block in zip(gathered, held)]
    ours, theirs, pending = [], [], []
    count = len(chains)
    for s in range(1, chips):
        for k, (_, step) in enumerate(chains):
            held[k] = shift(held[k], step)
            gathered[k] = keep(gathered[k], held[k], chip_behind(step, s))
        if s == 1:
            held[0], weight_grad = lax.optimization_barrier((held[0], weight_grad))
        if pending:
            *held, done = lax.optimization_barrier((*held, pending.pop()))
            if len(theirs) < count:
                theirs.append(swap(done))
            else:
                ours.append(done)
        else:
            held = list(lax.optimization_barrier(tuple(held)))
        at = s - 2
        if 0 <= at < 2 * count:
            k, half = at % count, at // count
            both = (*held, ordered)
            *held, rows_now = lax.optimization_barrier(both)
            first = chains[k][0]
            out = lax.dot_general(
                rows_now[half * chips * rows : (half + 1) * chips * rows],
                weight[first : first + piece],
                nt,
                preferred_element_type=jnp.float32,
            )
            out = out.astype(jnp.bfloat16).reshape(chips, rows, piece)
            pending.append(out)

    def term(k, chip):
        return take(ours[k], chip).astype(jnp.float32) + take(theirs[k], chip).astype(jnp.float32)

    sums = []
    for k, (_, step) in enumerate(chains):
        first = term(k, chip_behind(step, 1)).astype(jnp.bfloat16)
        first, held[k] = lax.optimization_barrier((first, held[k]))
        sums.append(first)
    others = []
    for s in range(1, chips):
        arrived = [shift(sums[k], step) for k, (_, step) in enumerate(chains)]
        arrived = lax.optimization_barrier(tuple(arrived))
        for k, (_, step) in enumerate(chains):
            total = arrived[k].astype(jnp.float32)
            total = total + term(k, chip_behind(step, (s + 1) % chips))
            if s == chips - 1:
                total = total + 0.5 * own[k].astype(jnp.float32)
            sums[k] = total.astype(jnp.bfloat16)
        k = s - 2
        if 0 <= k < count:
            sums[k], block = lax.optimization_barrier((sums[k], others[k]))
            block = gathered[k].at[0].set(block).reshape(n * rows, piece)
            block = lax.dot_general(block, ordered, tn, preferred_element_type=jnp.float32)
            weight_grad = lax.dynamic_update_slice(weight_grad, block * scale, (chains[k][0], 0))
        k = s - 1
        if k < count:
            sums[k], mine = lax.optimization_barrier((sums[k], gathered[k][1]))
            others.append(swap(mine))
    hidden_grad = jnp.concatenate(sums, axis=1)
    return (hidden_grad, weight_grad)


def solution(mesh):
    n, n_tp = mesh.shape["fsdp"], mesh.shape["tp"]
    placed = (P("fsdp", "tp"), P("tp", "fsdp"), P("tp", "fsdp"))
    return jax.shard_map(
        lambda *args: local(n, n_tp, *args),
        mesh=mesh,
        in_specs=placed,
        out_specs=(P("fsdp", "tp"), P("tp", "fsdp")),
        check_vma=False,
    )
```
